32 devices in a mesh: ens: 2 (over y), lat: 16 (over z, x, core).
Axes of the slice: x: 2, y: 2, z: 4, core: 2. Of those that a mesh axis runs over, the one named last changes fastest.
Arguments:
- signal: bfloat16 [32, 1440, 256], P(('ens', 'lat')), parts along dimension 0, may hold values from -6 to 6
- cotangent: bfloat16 [32, 1440, 256], P(('ens', 'lat')), parts along dimension 0, may hold values from -6 to 6
- weights: bfloat16 [2304, 256], replicated, may hold values from -0.125 to 0.125
- first_row: int32 [16], replicated, may hold values from -2 to -1, as said below
- last_row: int32 [16], replicated, may hold values from 1 to 2, as said below
- lon_reach: int32 [16], replicated, may hold values from 1 to 3, as said below
- basis_index: int32 [16, 5, 7], replicated, may hold values from 0 to 8
- quad_weight: float32 [16, 5, 7], replicated, may hold values from 0.2 to 1
Outputs:
- output: bfloat16 [32, 1440, 256], P(('ens', 'lat')), parts along dimension 0
- signal_grad: bfloat16 [32, 1440, 256], P(('ens', 'lat')), parts along dimension 0
- weight_grad: float32 [4608, 256], P(('ens', 'lat')), parts along dimension 0
The draws below stay inside these ranges and needn't reach their ends.
There are 2 independent parts, one for each index of `ens`. The reference program is written for one: setup_inputs(seed, part) draws one part's arguments, and reference() takes and returns one part's arrays. A program takes and returns all parts, laid end to end along the dimension named above; an argument that names none is the same for every part. Nothing has to cross between parts.
Inputs may be any that keep to these rules, and one draw needn't show every extreme that they name: Rows within 2 of either end of the grid have first_row = -2. Rows within 2 of either end of the grid have last_row = 2. Rows within 2 of either end of the grid have lon_reach = 3.
All inputs are finite; a program needn't handle non-finite values.
Results may differ from the reference program's by a relative error of at most 0.0058.
Values may be sent and summed in bfloat16 or wider, within the bound.
No kernel may reach another device: no remote copies, remote signals or barrier semaphores. Data moves between devices by JAX's collectives and lax.ppermute only.
A program may use at most 384 MiB of HBM per device.

```python
import math
import jax
import jax.numpy as jnp
from jax import lax

C = 256
K = 9
NLON = 1440
HALO = 2
REACH = 3
NLAT = 16
DEPTH = 5
NOFF = 7
POLAR = 2


def draw_first_row(key, part):
    row_ids = jnp.arange(NLAT, dtype=jnp.int32)
    polar_band = (row_ids < POLAR) | (row_ids >= NLAT - POLAR)
    random_depth = jax.random.randint(jax.random.fold_in(key, 11), (NLAT,), 1, HALO + 1, dtype=jnp.int32)
    return jnp.where(polar_band, -HALO, -random_depth).astype(jnp.int32)


def draw_last_row(key, part):
    row_ids = jnp.arange(NLAT, dtype=jnp.int32)
    polar_band = (row_ids < POLAR) | (row_ids >= NLAT - POLAR)
    random_depth = jax.random.randint(jax.random.fold_in(key, 23), (NLAT,), 1, HALO + 1, dtype=jnp.int32)
    return jnp.where(polar_band, HALO, random_depth).astype(jnp.int32)


def draw_lon_reach(key, part):
    row_ids = jnp.arange(NLAT, dtype=jnp.int32)
    polar_band = (row_ids < POLAR) | (row_ids >= NLAT - POLAR)
    random_reach = jax.random.randint(jax.random.fold_in(key, 37), (NLAT,), 1, REACH + 1, dtype=jnp.int32)
    return jnp.where(polar_band, REACH, random_reach).astype(jnp.int32)


def set_ends(result, own_key, low, high):
    dims = result.shape
    spot = [jax.random.randint(jax.random.fold_in(own_key, axis), (), 0, dims[axis]) for axis in range(len(dims))]
    result = result.at[tuple(spot)].set(low)
    longest = dims.index(max(dims))
    spot[longest] = (spot[longest] + 1) % dims[longest]
    return result.at[tuple(spot)].set(high)


def level_of(own_key, extent, cuts, least, top_value):
    level, own = 1.0, jax.random.fold_in(own_key, 6)
    for axis_at, parts in cuts:
        steps = jnp.exp(jax.random.uniform(jax.random.fold_in(own, axis_at), (parts,), jnp.float32, least / len(cuts), top_value / len(cuts)))
        level = level * jnp.repeat(steps, extent[axis_at] // parts).reshape([-1 if axis == axis_at else 1 for axis in range(len(extent))])
    return level


def gaussian(key, dims, scale, reach, pieces=(), kind=jnp.bfloat16):
    values = scale * jax.random.normal(key, dims, jnp.float32)
    if pieces:
        values = values * level_of(key, dims, pieces, -0.22, 0.18)
    return jnp.clip(values, -reach, reach).astype(kind)


def setup_inputs(seed: int = 0, part: int = 0) -> dict:
    key_list = jax.random.split(jax.random.key(seed), 9)
    part_splits = jax.random.split(jax.random.fold_in(key_list[8], part), 9)
    return {
        "signal": gaussian(part_splits[0], (NLAT, NLON, C), 1.0, 6.0, ((0, 16),)),
        "cotangent": gaussian(part_splits[1], (NLAT, NLON, C), 1.0, 6.0, ((0, 16),)),
        "weights": gaussian(key_list[2], (K * C, C), (K * C) ** -0.5, 0.125),
        "first_row": draw_first_row(jax.random.fold_in(key_list[8], 71), part),
        "last_row": draw_last_row(jax.random.fold_in(key_list[8], 71), part),
        "lon_reach": draw_lon_reach(jax.random.fold_in(key_list[8], 71), part),
        "basis_index": set_ends(jax.random.randint(key_list[6], (NLAT, DEPTH, NOFF), 0, K), jax.random.fold_in(key_list[6], 1), 0, K - 1).astype(jnp.int32),
        "quad_weight": jnp.clip(jax.random.uniform(key_list[7], (NLAT, DEPTH, NOFF), jnp.float32, 0.2, 1.0), 0.2, 1.0),
    }


def filters(first_row, last_row, lon_reach, basis_index, quad_weight):
    depth_pos = jnp.arange(2 * HALO + 1, dtype=jnp.int32) - HALO
    offset_pos = jnp.arange(2 * REACH + 1, dtype=jnp.int32) - REACH
    inside = (depth_pos[None, :, None] >= first_row[:, None, None]) & (depth_pos[None, :, None] <= last_row[:, None, None]) & (jnp.abs(offset_pos)[None, None, :] <= lon_reach[:, None, None])
    chosen = basis_index[:, :, None, :] == jnp.arange(K, dtype=jnp.int32)[None, None, :, None]
    kept_taps = inside[:, :, None, :] & chosen
    return jnp.where(kept_taps, quad_weight[:, :, None, :], 0.0).astype(jnp.bfloat16)

def reference(signal, cotangent, weights, first_row, last_row, lon_reach, basis_index, quad_weight):
    lat_rows, lon_cells, channels = signal.shape
    filter_table = filters(first_row, last_row, lon_reach, basis_index, quad_weight)
    depth_rows = 2 * HALO + 1
    tap_count = 2 * REACH + 1
    padded = jnp.pad(signal, ((HALO, HALO), (0, 0), (0, 0)))
    scale_factor = 1.0 / math.sqrt(lat_rows * lon_cells)

    def row_step(carried, row_index):
        weight_sum, window_sum = carried
        window = lax.dynamic_slice_in_dim(padded, row_index, depth_rows, 0).astype(jnp.float32)
        rolled = jnp.stack([jnp.roll(window, REACH - offset, axis=1) for offset in range(tap_count)])
        kernel = lax.dynamic_index_in_dim(filter_table, row_index, 0, keepdims=False).astype(jnp.float32)
        mixed_row = jnp.einsum('odjc,dko->jkc', rolled, kernel).astype(jnp.bfloat16).reshape(lon_cells, K * channels)
        output = jnp.dot(mixed_row, weights, preferred_element_type=jnp.float32).astype(jnp.bfloat16)
        upstream = lax.dynamic_index_in_dim(cotangent, row_index, 0, keepdims=False)
        weight_sum = weight_sum + lax.dot_general(mixed_row, upstream, (((0,), (0,)), ((), ())), preferred_element_type=jnp.float32)
        back_row = lax.dot_general(upstream, weights, (((1,), (1,)), ((), ())), preferred_element_type=jnp.float32)
        back_row = back_row.astype(jnp.bfloat16).reshape(lon_cells, K, channels).astype(jnp.float32)
        shifted = jnp.stack([jnp.roll(back_row, offset - REACH, axis=0) for offset in range(tap_count)])
        spread = jnp.einsum('ojkc,dko->djc', shifted, kernel)
        current = lax.dynamic_slice_in_dim(window_sum, row_index, depth_rows, 0)
        window_sum = lax.dynamic_update_slice_in_dim(window_sum, current + spread, row_index, 0)
        return ((weight_sum, window_sum), output)
    initial = (jnp.zeros((K * channels, channels), jnp.float32), jnp.zeros((lat_rows + 2 * HALO, lon_cells, channels), jnp.float32))
    (weight_sum, window_sum), output = lax.scan(row_step, initial, jnp.arange(lat_rows, dtype=jnp.int32))
    signal_grad = window_sum[HALO:HALO + lat_rows].astype(jnp.bfloat16)
    return (output, signal_grad, weight_sum * scale_factor)
```

```python
import functools
import math

import jax
import jax.numpy as jnp
from jax import lax
from jax.experimental import pallas as pl
from jax.experimental.pallas import tpu as pltpu
from jax.sharding import PartitionSpec as P

K = 9
HALO = 2
REACH = 3
DEPTH = 2 * HALO + 1
NOFF = 2 * REACH + 1
BLOCK = 32
WINDOW = 48
SHIFT = 8


def band_matrix(backward, meta, first, last, reach, basis, quad, band32, band):
    row, rows = meta[DEPTH], meta[DEPTH + 1]
    band32[...] = jnp.zeros_like(band32)
    shape = band32.shape[1:]
    diagonal = lax.broadcasted_iota(jnp.int32, shape, 1) - lax.broadcasted_iota(jnp.int32, shape, 0)
    for slot in range(DEPTH):
        place = meta[slot]
        source = row + place - HALO if backward else row
        depth = DEPTH - 1 - place if backward else place
        on_grid = (source >= 0) & (source < rows)
        source = jnp.clip(source, 0, rows - 1)
        inside = on_grid & (depth - HALO >= first[source]) & (depth - HALO <= last[source])
        for step in range(NOFF):
            offset = NOFF - 1 - step if backward else step
            at = (source * DEPTH + depth) * NOFF + offset
            kept = inside & (abs(offset - REACH) <= reach[source])
            value = jnp.where(kept, quad[at], 0.0)
            which = basis[at]
            hit = diagonal == slot * WINDOW + SHIFT - REACH + step
            band32[which] = band32[which] + jnp.where(hit, value, 0.0)
    band[...] = band32[...].reshape(band.shape).astype(band.dtype)


def layer_kernel(backward, *refs):
    scalars, refs = refs[:6], refs[6:]
    slots, refs = refs[:DEPTH], refs[DEPTH:]
    if backward:
        weights, out, band32, band, mixed, shifted = refs
    else:
        weights, turned, out, grad, band32, band, mixed, shifted = refs
    cells, width = out.shape
    band_matrix(backward, *scalars, band32, band)

    def mix(begin, window):
        result = jnp.dot(band[...], window, preferred_element_type=jnp.float32).astype(jnp.bfloat16)
        for k in range(K):
            mixed[pl.ds(begin, BLOCK), k * width : (k + 1) * width] = result[k * BLOCK : (k + 1) * BLOCK]

    @pl.loop(0, cells // BLOCK - 1, unroll=4)
    def _(block):
        begin = pl.multiple_of(block * BLOCK, BLOCK)
        mix(begin, jnp.concatenate([slot[pl.ds(begin, WINDOW), :] for slot in slots], axis=0))

    begin = cells - BLOCK
    pieces = []
    for slot in slots:
        pieces += [slot[begin:, :], slot[: WINDOW - BLOCK, :]]
    mix(begin, jnp.concatenate(pieces, axis=0))

    tile = cells // 5

    @pl.loop(0, 5)
    def _(part):
        begin = pl.multiple_of(part * tile, BLOCK)
        shifted[pl.ds(begin + SHIFT, tile), :] = jnp.dot(
            mixed[pl.ds(begin, tile), :], weights[...], preferred_element_type=jnp.float32
        )

    shifted[:SHIFT] = shifted[cells:]
    for part in range(5):
        out[part * tile : (part + 1) * tile, :] = shifted[part * tile : (part + 1) * tile].astype(out.dtype)
    if not backward:
        for k in range(K):
            term = jnp.dot(
                turned[...], mixed[:, k * width : (k + 1) * width], preferred_element_type=jnp.float32
            )
            grad[k * width : (k + 1) * width, :] = term.T.astype(grad.dtype)


def layer(backward, scalars, slots, weights, turned=None):
    cells, width = slots[0].shape
    outs = [jax.ShapeDtypeStruct((cells, width), jnp.bfloat16)]
    operands = [*slots, weights]
    if not backward:
        outs.append(jax.ShapeDtypeStruct(weights.shape, jnp.bfloat16))
        operands.append(turned)
    smem = pl.BlockSpec(memory_space=pltpu.SMEM)
    vmem = pl.BlockSpec(memory_space=pltpu.VMEM)
    return pl.pallas_call(
        functools.partial(layer_kernel, backward),
        out_shape=outs,
        in_specs=[smem] * 6 + [vmem] * len(operands),
        out_specs=[vmem] * len(outs),
        scratch_shapes=[
            pltpu.VMEM((K, BLOCK, DEPTH * WINDOW), jnp.float32),
            pltpu.VMEM((K * BLOCK, DEPTH * WINDOW), jnp.bfloat16),
            pltpu.VMEM((cells, K * width), jnp.bfloat16),
            pltpu.VMEM((cells + SHIFT, width), jnp.float32),
        ],
        compiler_params=pltpu.CompilerParams(vmem_limit_bytes=40 * 1024 * 1024),
        cost_estimate=pl.CostEstimate(
            flops=2 * cells * K * width * width * (2 if backward else 3),
            bytes_accessed=8 * cells * width * 2,
            transcendentals=0,
        ),
        name="backward_layer" if backward else "forward_layer",
    )(*scalars, *operands)


def shards(signal, cotangent, weights, first_row, last_row, lon_reach, basis_index, quad_weight):
    own_rows, cells, width = signal.shape
    assert own_rows == 1
    devices = lax.axis_size("lat")
    device = lax.axis_index("lat")
    core, side = device % 2, (device // 2) % 2
    across = [(i, i ^ 2) for i in range(devices)]
    cores = [(i, i ^ 1) for i in range(devices)]
    onward = [(i, i + 4) for i in range(devices) if not i & 2 and i + 4 < devices]
    onward += [(i, i - 4) for i in range(devices) if i & 2 and i >= 4]

    def sent(array, pairs):
        return lax.ppermute(array, "lat", pairs)

    meta = jnp.stack(
        [
            jnp.int32(HALO),
            jnp.where(core == 0, HALO + 1, HALO - 1),
            jnp.where(side == 0, 2 * HALO, 0),
            jnp.where(side == 0, 0, 2 * HALO),
            jnp.where(core == 0, HALO - 1, HALO + 1),
            device,
            jnp.int32(devices),
        ]
    ).astype(jnp.int32)
    scalars = [meta, first_row, last_row, lon_reach, basis_index.reshape(-1), quad_weight.reshape(-1)]

    def gathered(row):
        far = sent(row, across)
        beside = sent(row, cores)
        farther = sent(far, onward)
        extra = sent(jnp.where(side == core, far, farther), cores)
        return [row, beside, far, farther, extra]

    signal, cotangent = signal[0], cotangent[0]
    signal_rows = gathered(signal)
    cotangent_rows = gathered(cotangent)
    turned = jnp.roll(cotangent, -SHIFT, 0).T
    weights_back = weights.reshape(K, width, width).swapaxes(1, 2).reshape(K * width, width)

    output, share = layer(False, scalars, signal_rows, weights, turned)
    (signal_grad,) = layer(True, scalars, cotangent_rows, weights_back)

    share = share.reshape(devices, -1, width)
    bit = 1
    while bit < devices:
        part = (device // bit) % 2
        pairs = share.reshape(share.shape[0] // 2, 2, *share.shape[1:])
        kept = lax.dynamic_index_in_dim(pairs, part, 1, keepdims=False)
        given = lax.dynamic_index_in_dim(pairs, 1 - part, 1, keepdims=False)
        arrived = sent(given, [(i, i ^ bit) for i in range(devices)])
        share = kept.astype(jnp.float32) + arrived.astype(jnp.float32)
        bit *= 2
        if bit < devices:
            share = share.astype(jnp.bfloat16)
    weight_grad = share[0] * (1.0 / math.sqrt(devices * cells))
    return output[None], signal_grad[None], weight_grad


def solution(mesh):
    rows = P(("ens", "lat"), None, None)
    return jax.shard_map(
        shards,
        mesh=mesh,
        in_specs=(rows, rows, P(), P(), P(), P(), P(), P()),
        out_specs=(rows, rows, P(("ens", "lat"), None)),
        check_vma=False,
    )
```

```python
import functools
import math

import jax
import jax.numpy as jnp
from jax import lax
from jax.experimental import pallas as pl
from jax.experimental.pallas import tpu as pltpu
from jax.sharding import PartitionSpec as P

K = 9
HALO = 2
REACH = 3
DEPTH = 2 * HALO + 1
NOFF = 2 * REACH + 1
BLOCK = 32
WINDOW = 48
WRAP = WINDOW - BLOCK
COST = 5_000_000_000
LIMIT = 60
TILES = 5
TIE = 1
LATE = 4
HOLD = True
CUTS_F = ()
CUTS_B = ()
SHIFT = 8


def bands_kernel(meta, first, last, reach, basis, quad, *refs):
    band32 = refs[-1]
    shape = band32.shape[1:]
    diagonal = lax.broadcasted_iota(jnp.int32, shape, 1) - lax.broadcasted_iota(jnp.int32, shape, 0)
    row, rows = meta[DEPTH], meta[DEPTH + 1]
    for backward, band in enumerate(refs[:-1]):
        band32[...] = jnp.zeros_like(band32)
        for slot in range(DEPTH):
            place = meta[slot]
            source = row + place - HALO if backward else row
            depth = DEPTH - 1 - place if backward else place
            on_grid = (source >= 0) & (source < rows)
            source = jnp.clip(source, 0, rows - 1)
            inside = on_grid & (depth - HALO >= first[source]) & (depth - HALO <= last[source])
            for step in range(NOFF):
                offset = NOFF - 1 - step if backward else step
                at = (source * DEPTH + depth) * NOFF + offset
                kept = inside & (abs(offset - REACH) <= reach[source])
                value = jnp.where(kept, quad[at], 0.0)
                which = basis[at]
                hit = diagonal == slot * WINDOW + SHIFT - REACH + step
                band32[which] = band32[which] + jnp.where(hit, value, 0.0)
        band[...] = band32[...].reshape(band.shape).astype(band.dtype)


SMEM = pl.BlockSpec(memory_space=pltpu.SMEM)
VMEM = pl.BlockSpec(memory_space=pltpu.VMEM)
ANY = pl.BlockSpec(memory_space=pl.ANY)
BAND = (K * BLOCK, DEPTH * WINDOW)


def params():
    return pltpu.CompilerParams(vmem_limit_bytes=LIMIT * 1024 * 1024)


def cost(flops):
    return pl.CostEstimate(flops=flops, bytes_accessed=flops // 100, transcendentals=0)


def bands(scalars):
    return pl.pallas_call(
        bands_kernel,
        out_shape=[jax.ShapeDtypeStruct(BAND, jnp.bfloat16)] * 2,
        in_specs=[SMEM] * 6,
        out_specs=[VMEM] * 2,
        scratch_shapes=[pltpu.VMEM((K, BLOCK, DEPTH * WINDOW), jnp.float32)],
        compiler_params=params(),
        name="bands",
    )(*scalars)


def window_copies(counts, pieces, slots, arrived):
    cells = slots.shape[1] - WRAP
    tile = cells // TILES
    groups, used = [], 0
    for part in range(TILES):
        low = part * tile + WRAP if part else 0
        high = (part + 1) * tile + WRAP
        copies = []
        for slot, count in enumerate(counts):
            begin = 0
            moves = []
            for piece in pieces[sum(counts[:slot]) :][:count]:
                end = begin + piece.shape[0]
                first, last = max(low, begin), min(high, end)
                if first < last:
                    moves.append((piece.at[pl.ds(first - begin, last - first)], first))
                if begin == 0 and high > cells:
                    moves.append((piece.at[pl.ds(0, WRAP)], cells))
                begin = end
            for source, at in moves:
                target = slots.at[slot, pl.ds(at, source.shape[0])]
                copies.append(pltpu.make_async_copy(source, target, arrived.at[used]))
                used += 1
        groups.append(copies)
    return groups


def mix(band, slots, mixed, begin, blocks):
    width = slots.shape[2]

    @pl.loop(0, blocks, unroll=3)
    def _(block):
        at = pl.multiple_of(begin + block * BLOCK, BLOCK)
        window = jnp.concatenate([slots[slot, pl.ds(at, WINDOW), :] for slot in range(DEPTH)], axis=0)
        result = jnp.dot(band[...], window, preferred_element_type=jnp.float32).astype(jnp.bfloat16)
        for k in range(K):
            mixed[pl.ds(at, BLOCK), k * width : (k + 1) * width] = result[k * BLOCK : (k + 1) * BLOCK]


def layer_kernel(counts, meta, *refs):
    pieces, refs = refs[: sum(counts)], refs[sum(counts) :]
    *given, mixed, shifted, slots, weights, turned, grad, arrived, fetched = refs
    band, weights_in, *given = given
    turned_in, out, *grads = given if len(given) > 1 else (None, *given)
    cells, width = out.shape
    tile = cells // TILES
    groups = window_copies(counts, pieces, slots, arrived)
    fetches = [pltpu.make_async_copy(weights_in, weights, fetched.at[0])]
    if grads:
        fetches.append(pltpu.make_async_copy(turned_in, turned, fetched.at[1]))
    for copy in groups[0]:
        copy.start()
    for copy in fetches:
        copy.start()
    for copies in groups[1:]:
        for copy in copies:
            copy.start()
    for part in range(TILES):
        for copy in groups[part]:
            copy.wait()
        mix(band, slots, mixed, part * tile, tile // BLOCK)
        if part == 0:
            for copy in fetches:
                copy.wait()
        shifted[part * tile + SHIFT : (part + 1) * tile + SHIFT] = jnp.dot(
            mixed[part * tile : (part + 1) * tile], weights[...], preferred_element_type=jnp.float32
        )
    shifted[:SHIFT] = shifted[cells:]
    for part in range(TILES):
        out[part * tile : (part + 1) * tile, :] = shifted[part * tile : (part + 1) * tile].astype(out.dtype)
    if not grads:
        return
    target = grads[0] if len(grads) == 1 else grad
    for k in range(K):
        term = jnp.dot(turned[...], mixed[:, k * width : (k + 1) * width], preferred_element_type=jnp.float32)
        target[k * width : (k + 1) * width, :] = term.T.astype(grad.dtype)
    if len(grads) == 2:
        core = meta[DEPTH] % 2
        lines = grads[0].shape[1]
        for pair in range(grads[0].shape[0]):
            for which, array in enumerate(grads):
                other = core if which == 0 else 1 - core
                at = pl.multiple_of((2 * pair + other) * lines, 16)
                array[pair] = grad[pl.ds(at, lines), :]


def layer(meta, band, slots, weights, devices, turned=None):
    width = weights.shape[1]
    cells = sum(piece.shape[0] for piece in slots[0])
    counts = tuple(len(slot) for slot in slots)
    pieces = [piece for slot in slots for piece in slot]
    lines = K * width // devices
    outs = [jax.ShapeDtypeStruct((cells, width), jnp.bfloat16)]
    operands = [weights]
    if turned is not None:
        operands.append(turned)
        if lines % 16 == 0:
            outs += [jax.ShapeDtypeStruct((devices // 2, lines, width), jnp.bfloat16)] * 2
        else:
            outs += [jax.ShapeDtypeStruct((K * width, width), jnp.bfloat16)]
    out, *grads = pl.pallas_call(
        functools.partial(layer_kernel, counts),
        out_shape=outs,
        in_specs=[SMEM] + [ANY] * len(pieces) + [VMEM] + [ANY] * len(operands),
        out_specs=[VMEM] * len(outs),
        scratch_shapes=[
            pltpu.VMEM((cells, K * width), jnp.bfloat16),
            pltpu.VMEM((cells + SHIFT, width), jnp.float32),
            pltpu.VMEM((DEPTH, cells + WRAP, width), jnp.bfloat16),
            pltpu.VMEM(weights.shape, jnp.bfloat16),
            pltpu.VMEM((width, cells), jnp.bfloat16),
            pltpu.VMEM((K * width, width), jnp.bfloat16),
            pltpu.SemaphoreType.DMA((TILES * 2 * len(pieces),)),
            pltpu.SemaphoreType.DMA((2,)),
        ],
        compiler_params=params(),
        cost_estimate=cost(COST),
        name="backward_layer" if turned is None else "forward_layer",
    )(meta, *pieces, band, *operands)
    if len(grads) == 1:
        parts = grads[0].reshape(devices // 2, 2, lines, width)
        core = meta[DEPTH] % 2
        grads = [lax.dynamic_index_in_dim(parts, at, 1, keepdims=False) for at in (core, 1 - core)]
    return out, *grads


def shards(signal, cotangent, weights, first_row, last_row, lon_reach, basis_index, quad_weight):
    own_rows, cells, width = signal.shape
    assert own_rows == 1
    devices = lax.axis_size("lat")
    device = lax.axis_index("lat")
    core, side = device % 2, (device // 2) % 2
    across = [(i, i ^ 2) for i in range(devices)]
    cores = [(i, i ^ 1) for i in range(devices)]
    onward = [(i, i + 4) for i in range(devices) if not i & 2 and i + 4 < devices]
    onward += [(i, i - 4) for i in range(devices) if i & 2 and i >= 4]

    def sent(array, pairs):
        return lax.ppermute(array, "lat", pairs)

    meta = jnp.stack(
        [
            jnp.int32(HALO),
            jnp.where(core == 0, HALO + 1, HALO - 1),
            jnp.where(side == 0, 2 * HALO, 0),
            jnp.where(side == 0, 0, 2 * HALO),
            jnp.where(core == 0, HALO - 1, HALO + 1),
            device,
            jnp.int32(devices),
        ]
    ).astype(jnp.int32)
    scalars = [meta, first_row, last_row, lon_reach, basis_index.reshape(-1), quad_weight.reshape(-1)]

    def split(row, cuts):
        edges = [0, *cuts, cells]
        return [row[low:high] for low, high in zip(edges, edges[1:])]

    def swapped(far, farther):
        return [sent(jnp.where(side == core, one, other), cores) for one, other in zip(far, farther)]

    signal, cotangent = signal[0], cotangent[0]
    turned = jnp.roll(cotangent, -SHIFT, 0).T
    weights_back = weights.reshape(K, width, width).swapaxes(1, 2).reshape(K * width, width)

    first_piece, *later = split(signal, CUTS_F)
    signal_far = [sent(first_piece, across)]
    if later:
        signal_far[0], later, cotangent_sent = lax.optimization_barrier((signal_far[0], later, cotangent))
    else:
        cotangent_sent = cotangent
    signal_far += [sent(piece, across) for piece in later]
    cotangent_far = [sent(piece, across) for piece in split(cotangent_sent, CUTS_B)]
    signal_beside, cotangent_beside = sent(signal, cores), sent(cotangent, cores)
    ready = (turned, weights_back, bands(scalars), signal_beside, cotangent_beside)
    signal_far[0], ready = lax.optimization_barrier((signal_far[0], ready))
    turned, weights_back, (band, band_back), signal_beside, cotangent_beside = ready
    signal_farther = [sent(piece, onward) for piece in signal_far]
    cotangent_farther = [sent(piece, onward) for piece in cotangent_far]
    if HOLD:
        signal_farther, _ = lax.optimization_barrier((signal_farther, cotangent_far))
    signal_extra = swapped(signal_far, signal_farther)
    signal_rows = [[signal], [signal_beside], signal_far, signal_farther, signal_extra]
    cotangent_rows = [[cotangent], [cotangent_beside], cotangent_far, cotangent_farther, None]

    output, kept, given = layer(meta, band, signal_rows, weights, devices, turned)
    bit = 1
    while True:
        if bit == TIE:
            given, cotangent_rows[3] = lax.optimization_barrier((given, cotangent_rows[3]))
        arrived = sent(given, [(i, i ^ bit) for i in range(devices)])
        share = kept.astype(jnp.float32) + arrived.astype(jnp.float32)
        bit *= 2
        if bit == devices:
            break
        share = share.astype(jnp.bfloat16)
        if bit == TIE * 2 or TIE == 0 and bit == 2:
            cotangent_rows[4] = swapped(cotangent_far, cotangent_rows[3])
            (signal_grad,) = layer(meta, band_back, cotangent_rows, weights_back, devices)
        if bit == LATE:
            share, signal_grad = lax.optimization_barrier((share, signal_grad))
        parts = share.reshape(share.shape[0] // 2, 2, *share.shape[1:])
        part = (device // bit) % 2
        kept = lax.dynamic_index_in_dim(parts, part, 1, keepdims=False)
        given = lax.dynamic_index_in_dim(parts, 1 - part, 1, keepdims=False)
    weight_grad = share[0] * (1.0 / math.sqrt(devices * cells))
    return output[None], signal_grad[None], weight_grad


def solution(mesh):
    rows = P(("ens", "lat"), None, None)
    return jax.shard_map(
        shards,
        mesh=mesh,
        in_specs=(rows, rows, P(), P(), P(), P(), P(), P()),
        out_specs=(rows, rows, P(("ens", "lat"), None)),
        check_vma=False,
    )
```

```python
import functools
import math

import jax
import jax.numpy as jnp
from jax import lax
from jax.experimental import pallas as pl
from jax.experimental.pallas import tpu as pltpu
from jax.sharding import PartitionSpec as P

K = 9
HALO = 2
REACH = 3
DEPTH = 2 * HALO + 1
NOFF = 2 * REACH + 1
BLOCK = 32
WINDOW = 48
WRAP = WINDOW - BLOCK
COST = 5_000_000_000
LIMIT = 60
FCOST = 1
TILES = 3
TIE = 1
LATE = 4
HOLD = True
CUTS_F = (720,)
CUTS_B = ()
SHIFT = 8


def bands_kernel(meta, first, last, reach, basis, quad, *refs):
    band32 = refs[-1]
    shape = band32.shape[1:]
    diagonal = lax.broadcasted_iota(jnp.int32, shape, 1) - lax.broadcasted_iota(jnp.int32, shape, 0)
    row, rows = meta[DEPTH], meta[DEPTH + 1]
    for backward, band in enumerate(refs[:-1]):
        band32[...] = jnp.zeros_like(band32)
        for slot in range(DEPTH):
            place = meta[slot]
            source = row + place - HALO if backward else row
            depth = DEPTH - 1 - place if backward else place
            on_grid = (source >= 0) & (source < rows)
            source = jnp.clip(source, 0, rows - 1)
            inside = on_grid & (depth - HALO >= first[source]) & (depth - HALO <= last[source])
            for step in range(NOFF):
                offset = NOFF - 1 - step if backward else step
                at = (source * DEPTH + depth) * NOFF + offset
                kept = inside & (abs(offset - REACH) <= reach[source])
                value = jnp.where(kept, quad[at], 0.0)
                which = basis[at]
                hit = diagonal == slot * WINDOW + SHIFT - REACH + step
                band32[which] = band32[which] + jnp.where(hit, value, 0.0)
        band[...] = band32[...].reshape(band.shape).astype(band.dtype)


SMEM = pl.BlockSpec(memory_space=pltpu.SMEM)
VMEM = pl.BlockSpec(memory_space=pltpu.VMEM)
ANY = pl.BlockSpec(memory_space=pl.ANY)
BAND = (K * BLOCK, DEPTH * WINDOW)


def params():
    return pltpu.CompilerParams(vmem_limit_bytes=LIMIT * 1024 * 1024)


def cost(flops):
    return pl.CostEstimate(flops=flops, bytes_accessed=flops // 100, transcendentals=0)


def bands(scalars):
    return pl.pallas_call(
        bands_kernel,
        out_shape=[jax.ShapeDtypeStruct(BAND, jnp.bfloat16)] * 2,
        in_specs=[SMEM] * 6,
        out_specs=[VMEM] * 2,
        scratch_shapes=[pltpu.VMEM((K, BLOCK, DEPTH * WINDOW), jnp.float32)],
        compiler_params=params(),
        name="bands",
    )(*scalars)


def window_copies(counts, pieces, slots, arrived):
    cells = slots.shape[1] - WRAP
    tile = cells // TILES
    groups, used = [], 0
    for part in range(TILES):
        low = part * tile + WRAP if part else 0
        high = (part + 1) * tile + WRAP
        copies = []
        for slot, count in enumerate(counts):
            begin = 0
            moves = []
            for piece in pieces[sum(counts[:slot]) :][:count]:
                end = begin + piece.shape[0]
                first, last = max(low, begin), min(high, end)
                if first < last:
                    moves.append((piece.at[pl.ds(first - begin, last - first)], first))
                if begin == 0 and high > cells:
                    moves.append((piece.at[pl.ds(0, WRAP)], cells))
                begin = end
            for source, at in moves:
                target = slots.at[slot, pl.ds(at, source.shape[0])]
                copies.append(pltpu.make_async_copy(source, target, arrived.at[used]))
                used += 1
        groups.append(copies)
    return groups


def mix(band, slots, mixed, begin, blocks):
    width = slots.shape[2]

    @pl.loop(0, blocks, unroll=5)
    def _(block):
        at = pl.multiple_of(begin + block * BLOCK, BLOCK)
        window = jnp.concatenate([slots[slot, pl.ds(at, WINDOW), :] for slot in range(DEPTH)], axis=0)
        result = jnp.dot(band[...], window, preferred_element_type=jnp.float32).astype(jnp.bfloat16)
        for k in range(K):
            mixed[pl.ds(at, BLOCK), k * width : (k + 1) * width] = result[k * BLOCK : (k + 1) * BLOCK]


def layer_kernel(counts, meta, *refs):
    pieces, refs = refs[: sum(counts)], refs[sum(counts) :]
    *given, mixed, shifted, slots, weights, turned, grad, arrived, fetched = refs
    band, weights_in, *given = given
    turned_in, out, *grads = given if len(given) > 1 else (None, *given)
    cells, width = out.shape
    tile = cells // TILES
    groups = window_copies(counts, pieces, slots, arrived)
    fetches = [pltpu.make_async_copy(weights_in, weights, fetched.at[0])]
    if grads:
        fetches.append(pltpu.make_async_copy(turned_in, turned, fetched.at[1]))
    for copy in groups[0]:
        copy.start()
    for copy in fetches:
        copy.start()
    for copies in groups[1:]:
        for copy in copies:
            copy.start()
    for part in range(TILES):
        for copy in groups[part]:
            copy.wait()
        mix(band, slots, mixed, part * tile, tile // BLOCK)
        if part == 0:
            for copy in fetches:
                copy.wait()
        shifted[part * tile + SHIFT : (part + 1) * tile + SHIFT] = jnp.dot(
            mixed[part * tile : (part + 1) * tile], weights[...], preferred_element_type=jnp.float32
        )
    shifted[:SHIFT] = shifted[cells:]
    for part in range(TILES):
        out[part * tile : (part + 1) * tile, :] = shifted[part * tile : (part + 1) * tile].astype(out.dtype)
    if not grads:
        return
    target = grads[0] if len(grads) == 1 else grad
    for k in range(K):
        term = jnp.dot(turned[...], mixed[:, k * width : (k + 1) * width], preferred_element_type=jnp.float32)
        target[k * width : (k + 1) * width, :] = term.T.astype(grad.dtype)
    if len(grads) == 2:
        core = meta[DEPTH] % 2
        lines = grads[0].shape[1]
        for pair in range(grads[0].shape[0]):
            for which, array in enumerate(grads):
                other = core if which == 0 else 1 - core
                at = pl.multiple_of((2 * pair + other) * lines, 16)
                array[pair] = grad[pl.ds(at, lines), :]


def layer(meta, band, slots, weights, devices, turned=None):
    width = weights.shape[1]
    cells = sum(piece.shape[0] for piece in slots[0])
    counts = tuple(len(slot) for slot in slots)
    pieces = [piece for slot in slots for piece in slot]
    lines = K * width // devices
    outs = [jax.ShapeDtypeStruct((cells, width), jnp.bfloat16)]
    operands = [weights]
    if turned is not None:
        operands.append(turned)
        if lines % 16 == 0:
            outs += [jax.ShapeDtypeStruct((devices // 2, lines, width), jnp.bfloat16)] * 2
        else:
            outs += [jax.ShapeDtypeStruct((K * width, width), jnp.bfloat16)]
    out, *grads = pl.pallas_call(
        functools.partial(layer_kernel, counts),
        out_shape=outs,
        in_specs=[SMEM] + [ANY] * len(pieces) + [VMEM] + [ANY] * len(operands),
        out_specs=[VMEM] * len(outs),
        scratch_shapes=[
            pltpu.VMEM((cells, K * width), jnp.bfloat16),
            pltpu.VMEM((cells + SHIFT, width), jnp.float32),
            pltpu.VMEM((DEPTH, cells + WRAP, width), jnp.bfloat16),
            pltpu.VMEM(weights.shape, jnp.bfloat16),
            pltpu.VMEM((width, cells), jnp.bfloat16),
            pltpu.VMEM((K * width, width), jnp.bfloat16),
            pltpu.SemaphoreType.DMA((TILES * 2 * len(pieces),)),
            pltpu.SemaphoreType.DMA((2,)),
        ],
        compiler_params=params(),
        cost_estimate=cost(COST if turned is None else FCOST),
        name="backward_layer" if turned is None else "forward_layer",
    )(meta, *pieces, band, *operands)
    if len(grads) == 1:
        parts = grads[0].reshape(devices // 2, 2, lines, width)
        core = meta[DEPTH] % 2
        grads = [lax.dynamic_index_in_dim(parts, at, 1, keepdims=False) for at in (core, 1 - core)]
    return out, *grads


def shards(signal, cotangent, weights, first_row, last_row, lon_reach, basis_index, quad_weight):
    own_rows, cells, width = signal.shape
    assert own_rows == 1
    devices = lax.axis_size("lat")
    device = lax.axis_index("lat")
    core, side = device % 2, (device // 2) % 2
    across = [(i, i ^ 2) for i in range(devices)]
    cores = [(i, i ^ 1) for i in range(devices)]
    onward = [(i, i + 4) for i in range(devices) if not i & 2 and i + 4 < devices]
    onward += [(i, i - 4) for i in range(devices) if i & 2 and i >= 4]

    def sent(array, pairs):
        return lax.ppermute(array, "lat", pairs)

    meta = jnp.stack(
        [
            jnp.int32(HALO),
            jnp.where(core == 0, HALO + 1, HALO - 1),
            jnp.where(side == 0, 2 * HALO, 0),
            jnp.where(side == 0, 0, 2 * HALO),
            jnp.where(core == 0, HALO - 1, HALO + 1),
            device,
            jnp.int32(devices),
        ]
    ).astype(jnp.int32)
    scalars = [meta, first_row, last_row, lon_reach, basis_index.reshape(-1), quad_weight.reshape(-1)]

    def split(row, cuts):
        edges = [0, *cuts, cells]
        return [row[low:high] for low, high in zip(edges, edges[1:])]

    def swapped(far, farther):
        return [sent(jnp.where(side == core, one, other), cores) for one, other in zip(far, farther)]

    signal, cotangent = signal[0], cotangent[0]
    turned = jnp.roll(cotangent, -SHIFT, 0).T
    weights_back = weights.reshape(K, width, width).swapaxes(1, 2).reshape(K * width, width)

    signal_far = [sent(piece, across) for piece in split(signal, CUTS_F)]
    signal_beside, cotangent_beside = sent(signal, cores), sent(cotangent, cores)
    ready = (turned, weights_back, bands(scalars), meta)
    if CUTS_F:
        signal_far[0], cotangent_sent, ready = lax.optimization_barrier((signal_far[0], cotangent, ready))
        cotangent_far = [sent(piece, across) for piece in split(cotangent_sent, CUTS_B)]
    else:
        cotangent_far = [sent(piece, across) for piece in split(cotangent, CUTS_B)]
        signal_far[0], ready = lax.optimization_barrier((signal_far[0], ready))
    turned, weights_back, (band, band_back), meta = ready
    signal_farther = [sent(piece, onward) for piece in signal_far]
    cotangent_farther = [sent(piece, onward) for piece in cotangent_far]
    if HOLD:
        signal_farther, _ = lax.optimization_barrier((signal_farther, cotangent_far))
    signal_extra = swapped(signal_far, signal_farther)
    signal_rows = [[signal], [signal_beside], signal_far, signal_farther, signal_extra]
    cotangent_rows = [[cotangent], [cotangent_beside], cotangent_far, cotangent_farther, None]

    output, kept, given = layer(meta, band, signal_rows, weights, devices, turned)
    bit = 1
    while True:
        if bit == TIE:
            given, cotangent_rows[3] = lax.optimization_barrier((given, cotangent_rows[3]))
        arrived = sent(given, [(i, i ^ bit) for i in range(devices)])
        share = kept.astype(jnp.float32) + arrived.astype(jnp.float32)
        bit *= 2
        if bit == devices:
            break
        share = share.astype(jnp.bfloat16)
        if bit == TIE * 2 or TIE == 0 and bit == 2:
            cotangent_rows[4] = swapped(cotangent_far, cotangent_rows[3])
            (signal_grad,) = layer(meta, band_back, cotangent_rows, weights_back, devices)
        if bit == LATE:
            share, signal_grad = lax.optimization_barrier((share, signal_grad))
        parts = share.reshape(share.shape[0] // 2, 2, *share.shape[1:])
        part = (device // bit) % 2
        kept = lax.dynamic_index_in_dim(parts, part, 1, keepdims=False)
        given = lax.dynamic_index_in_dim(parts, 1 - part, 1, keepdims=False)
    weight_grad = share[0] * (1.0 / math.sqrt(devices * cells))
    return output[None], signal_grad[None], weight_grad


def solution(mesh):
    rows = P(("ens", "lat"), None, None)
    return jax.shard_map(
        shards,
        mesh=mesh,
        in_specs=(rows, rows, P(), P(), P(), P(), P(), P()),
        out_specs=(rows, rows, P(("ens", "lat"), None)),
        check_vma=False,
    )
```

```python
import functools
import math

import jax
import jax.numpy as jnp
from jax import lax
from jax.experimental import pallas as pl
from jax.experimental.pallas import tpu as pltpu
from jax.sharding import PartitionSpec as P

K = 9
HALO = 2
REACH = 3
DEPTH = 2 * HALO + 1
NOFF = 2 * REACH + 1
BLOCK = 32
WINDOW = 48
WRAP = WINDOW - BLOCK
COST = 5_000_000_000
LIMIT = 60
FCOST = 1
TILES = 3
TIE = 1
LATE = 4
HOLD = True
CUTS_F = (720,)
CUTS_B = (960,)
SHIFT = 8


def bands_kernel(meta, first, last, reach, basis, quad, *refs):
    band32 = refs[-1]
    shape = band32.shape[1:]
    diagonal = lax.broadcasted_iota(jnp.int32, shape, 1) - lax.broadcasted_iota(jnp.int32, shape, 0)
    row, rows = meta[DEPTH], meta[DEPTH + 1]
    for backward, band in enumerate(refs[:-1]):
        band32[...] = jnp.zeros_like(band32)
        for slot in range(DEPTH):
            place = meta[slot]
            source = row + place - HALO if backward else row
            depth = DEPTH - 1 - place if backward else place
            on_grid = (source >= 0) & (source < rows)
            source = jnp.clip(source, 0, rows - 1)
            inside = on_grid & (depth - HALO >= first[source]) & (depth - HALO <= last[source])
            for step in range(NOFF):
                offset = NOFF - 1 - step if backward else step
                at = (source * DEPTH + depth) * NOFF + offset
                kept = inside & (abs(offset - REACH) <= reach[source])
                value = jnp.where(kept, quad[at], 0.0)
                which = basis[at]
                hit = diagonal == slot * WINDOW + SHIFT - REACH + step
                band32[which] = band32[which] + jnp.where(hit, value, 0.0)
        band[...] = band32[...].reshape(band.shape).astype(band.dtype)


SMEM = pl.BlockSpec(memory_space=pltpu.SMEM)
VMEM = pl.BlockSpec(memory_space=pltpu.VMEM)
ANY = pl.BlockSpec(memory_space=pl.ANY)
BAND = (K * BLOCK, DEPTH * WINDOW)


def params():
    return pltpu.CompilerParams(vmem_limit_bytes=LIMIT * 1024 * 1024)


def cost(flops):
    return pl.CostEstimate(flops=flops, bytes_accessed=flops // 100, transcendentals=0)


def bands(scalars):
    return pl.pallas_call(
        bands_kernel,
        out_shape=[jax.ShapeDtypeStruct(BAND, jnp.bfloat16)] * 2,
        in_specs=[SMEM] * 6,
        out_specs=[VMEM] * 2,
        scratch_shapes=[pltpu.VMEM((K, BLOCK, DEPTH * WINDOW), jnp.float32)],
        compiler_params=params(),
        name="bands",
    )(*scalars)


def window_copies(counts, pieces, slots, arrived):
    cells = slots.shape[1] - WRAP
    tile = cells // TILES
    groups, used = [], 0
    for part in range(TILES):
        low = part * tile + WRAP if part else 0
        high = (part + 1) * tile + WRAP
        copies = []
        for slot, count in enumerate(counts):
            begin = 0
            moves = []
            for piece in pieces[sum(counts[:slot]) :][:count]:
                end = begin + piece.shape[0]
                first, last = max(low, begin), min(high, end)
                if first < last:
                    moves.append((piece.at[pl.ds(first - begin, last - first)], first))
                if begin == 0 and high > cells:
                    moves.append((piece.at[pl.ds(0, WRAP)], cells))
                begin = end
            for source, at in moves:
                target = slots.at[slot, pl.ds(at, source.shape[0])]
                copies.append(pltpu.make_async_copy(source, target, arrived.at[used]))
                used += 1
        groups.append(copies)
    return groups


def mix(band, slots, mixed, begin, blocks):
    width = slots.shape[2]

    @pl.loop(0, blocks, unroll=5)
    def _(block):
        at = pl.multiple_of(begin + block * BLOCK, BLOCK)
        window = jnp.concatenate([slots[slot, pl.ds(at, WINDOW), :] for slot in range(DEPTH)], axis=0)
        result = jnp.dot(band[...], window, preferred_element_type=jnp.float32).astype(jnp.bfloat16)
        for k in range(K):
            mixed[pl.ds(at, BLOCK), k * width : (k + 1) * width] = result[k * BLOCK : (k + 1) * BLOCK]


def layer_kernel(counts, meta, *refs):
    pieces, refs = refs[: sum(counts)], refs[sum(counts) :]
    *given, mixed, shifted, slots, weights, turned, grad, arrived, fetched = refs
    band, weights_in, *given = given
    turned_in, out, *grads = given if len(given) > 1 else (None, *given)
    cells, width = out.shape
    tile = cells // TILES
    groups = window_copies(counts, pieces, slots, arrived)
    fetches = [pltpu.make_async_copy(weights_in, weights, fetched.at[0])]
    if grads:
        fetches.append(pltpu.make_async_copy(turned_in, turned, fetched.at[1]))
    for copy in groups[0]:
        copy.start()
    for copy in fetches:
        copy.start()
    for copies in groups[1:]:
        for copy in copies:
            copy.start()
    for part in range(TILES):
        for copy in groups[part]:
            copy.wait()
        mix(band, slots, mixed, part * tile, tile // BLOCK)
        if part == 0:
            for copy in fetches:
                copy.wait()
        shifted[part * tile + SHIFT : (part + 1) * tile + SHIFT] = jnp.dot(
            mixed[part * tile : (part + 1) * tile], weights[...], preferred_element_type=jnp.float32
        )
    shifted[:SHIFT] = shifted[cells:]
    for part in range(TILES):
        out[part * tile : (part + 1) * tile, :] = shifted[part * tile : (part + 1) * tile].astype(out.dtype)
    if not grads:
        return
    target = grads[0] if len(grads) == 1 else grad
    for k in range(K):
        term = jnp.dot(turned[...], mixed[:, k * width : (k + 1) * width], preferred_element_type=jnp.float32)
        target[k * width : (k + 1) * width, :] = term.T.astype(grad.dtype)
    if len(grads) == 2:
        core = meta[DEPTH] % 2
        lines = grads[0].shape[1]
        for pair in range(grads[0].shape[0]):
            for which, array in enumerate(grads):
                other = core if which == 0 else 1 - core
                at = pl.multiple_of((2 * pair + other) * lines, 16)
                array[pair] = grad[pl.ds(at, lines), :]


def layer(meta, band, slots, weights, devices, turned=None):
    width = weights.shape[1]
    cells = sum(piece.shape[0] for piece in slots[0])
    counts = tuple(len(slot) for slot in slots)
    pieces = [piece for slot in slots for piece in slot]
    lines = K * width // devices
    outs = [jax.ShapeDtypeStruct((cells, width), jnp.bfloat16)]
    operands = [weights]
    if turned is not None:
        operands.append(turned)
        if lines % 16 == 0:
            outs += [jax.ShapeDtypeStruct((devices // 2, lines, width), jnp.bfloat16)] * 2
        else:
            outs += [jax.ShapeDtypeStruct((K * width, width), jnp.bfloat16)]
    out, *grads = pl.pallas_call(
        functools.partial(layer_kernel, counts),
        out_shape=outs,
        in_specs=[SMEM] + [ANY] * len(pieces) + [VMEM] + [ANY] * len(operands),
        out_specs=[VMEM] * len(outs),
        scratch_shapes=[
            pltpu.VMEM((cells, K * width), jnp.bfloat16),
            pltpu.VMEM((cells + SHIFT, width), jnp.float32),
            pltpu.VMEM((DEPTH, cells + WRAP, width), jnp.bfloat16),
            pltpu.VMEM(weights.shape, jnp.bfloat16),
            pltpu.VMEM((width, cells), jnp.bfloat16),
            pltpu.VMEM((K * width, width), jnp.bfloat16),
            pltpu.SemaphoreType.DMA((TILES * 2 * len(pieces),)),
            pltpu.SemaphoreType.DMA((2,)),
        ],
        compiler_params=params(),
        cost_estimate=cost(COST if turned is None else FCOST),
        name="backward_layer" if turned is None else "forward_layer",
    )(meta, *pieces, band, *operands)
    if len(grads) == 1:
        parts = grads[0].reshape(devices // 2, 2, lines, width)
        core = meta[DEPTH] % 2
        grads = [lax.dynamic_index_in_dim(parts, at, 1, keepdims=False) for at in (core, 1 - core)]
    return out, *grads


def shards(signal, cotangent, weights, first_row, last_row, lon_reach, basis_index, quad_weight):
    own_rows, cells, width = signal.shape
    assert own_rows == 1
    devices = lax.axis_size("lat")
    device = lax.axis_index("lat")
    core, side = device % 2, (device // 2) % 2
    across = [(i, i ^ 2) for i in range(devices)]
    cores = [(i, i ^ 1) for i in range(devices)]
    onward = [(i, i + 4) for i in range(devices) if not i & 2 and i + 4 < devices]
    onward += [(i, i - 4) for i in range(devices) if i & 2 and i >= 4]

    def sent(array, pairs):
        return lax.ppermute(array, "lat", pairs)

    meta = jnp.stack(
        [
            jnp.int32(HALO),
            jnp.where(core == 0, HALO + 1, HALO - 1),
            jnp.where(side == 0, 2 * HALO, 0),
            jnp.where(side == 0, 0, 2 * HALO),
            jnp.where(core == 0, HALO - 1, HALO + 1),
            device,
            jnp.int32(devices),
        ]
    ).astype(jnp.int32)
    scalars = [meta, first_row, last_row, lon_reach, basis_index.reshape(-1), quad_weight.reshape(-1)]

    def split(row, cuts):
        edges = [0, *cuts, cells]
        return [row[low:high] for low, high in zip(edges, edges[1:])]

    def swapped(far, farther):
        return [sent(jnp.where(side == core, one, other), cores) for one, other in zip(far, farther)]

    signal, cotangent = signal[0], cotangent[0]
    turned = jnp.roll(cotangent, -SHIFT, 0).T
    weights_back = weights.reshape(K, width, width).swapaxes(1, 2).reshape(K * width, width)

    signal_far = [sent(piece, across) for piece in split(signal, CUTS_F)]
    signal_beside, cotangent_beside = sent(signal, cores), sent(cotangent, cores)
    ready = (turned, weights_back, bands(scalars), meta)
    if CUTS_F:
        signal_far[0], cotangent_sent, ready = lax.optimization_barrier((signal_far[0], cotangent, ready))
        cotangent_far = [sent(piece, across) for piece in split(cotangent_sent, CUTS_B)]
    else:
        cotangent_far = [sent(piece, across) for piece in split(cotangent, CUTS_B)]
        signal_far[0], ready = lax.optimization_barrier((signal_far[0], ready))
    turned, weights_back, (band, band_back), meta = ready
    signal_farther = [sent(piece, onward) for piece in signal_far]
    cotangent_farther = [sent(piece, onward) for piece in cotangent_far]
    if HOLD:
        signal_farther, _ = lax.optimization_barrier((signal_farther, cotangent_far[0]))
    signal_extra = swapped(signal_far, signal_farther)
    signal_rows = [[signal], [signal_beside], signal_far, signal_farther, signal_extra]
    cotangent_rows = [[cotangent], [cotangent_beside], cotangent_far, cotangent_farther, None]

    output, kept, given = layer(meta, band, signal_rows, weights, devices, turned)
    bit = 1
    while True:
        if bit == TIE:
            given, cotangent_rows[3] = lax.optimization_barrier((given, cotangent_rows[3]))
        arrived = sent(given, [(i, i ^ bit) for i in range(devices)])
        share = kept.astype(jnp.float32) + arrived.astype(jnp.float32)
        bit *= 2
        if bit == devices:
            break
        share = share.astype(jnp.bfloat16)
        if bit == TIE * 2 or TIE == 0 and bit == 2:
            cotangent_rows[4] = swapped(cotangent_far, cotangent_rows[3])
            (signal_grad,) = layer(meta, band_back, cotangent_rows, weights_back, devices)
        if bit == LATE:
            share, signal_grad = lax.optimization_barrier((share, signal_grad))
        parts = share.reshape(share.shape[0] // 2, 2, *share.shape[1:])
        part = (device // bit) % 2
        kept = lax.dynamic_index_in_dim(parts, part, 1, keepdims=False)
        given = lax.dynamic_index_in_dim(parts, 1 - part, 1, keepdims=False)
    weight_grad = share[0] * (1.0 / math.sqrt(devices * cells))
    return output[None], signal_grad[None], weight_grad


def solution(mesh):
    rows = P(("ens", "lat"), None, None)
    return jax.shard_map(
        shards,
        mesh=mesh,
        in_specs=(rows, rows, P(), P(), P(), P(), P(), P()),
        out_specs=(rows, rows, P(("ens", "lat"), None)),
        check_vma=False,
    )
```

```python
import functools
import math

import jax
import jax.numpy as jnp
from jax import lax
from jax.experimental import pallas as pl
from jax.experimental.pallas import tpu as pltpu
from jax.sharding import PartitionSpec as P

K = 9
HALO = 2
REACH = 3
DEPTH = 2 * HALO + 1
NOFF = 2 * REACH + 1
BLOCK = 32
WINDOW = 48
WRAP = WINDOW - BLOCK
COST = 5_000_000_000
LIMIT = 60
FCOST = 1
TILES = 3
TIE = 1
LATE = 4
HOLD = True
CUTS_F = (720,)
CUTS_B = (960,)
SHIFT = 8


def bands_kernel(meta, first, last, reach, basis, quad, *refs):
    band32 = refs[-1]
    shape = band32.shape[1:]
    diagonal = lax.broadcasted_iota(jnp.int32, shape, 1) - lax.broadcasted_iota(jnp.int32, shape, 0)
    row, rows = meta[DEPTH], meta[DEPTH + 1]
    for backward, band in enumerate(refs[:-1]):
        band32[...] = jnp.zeros_like(band32)
        for slot in range(DEPTH):
            place = meta[slot]
            source = row + place - HALO if backward else row
            depth = DEPTH - 1 - place if backward else place
            on_grid = (source >= 0) & (source < rows)
            source = jnp.clip(source, 0, rows - 1)
            inside = on_grid & (depth - HALO >= first[source]) & (depth - HALO <= last[source])
            for step in range(NOFF):
                offset = NOFF - 1 - step if backward else step
                at = (source * DEPTH + depth) * NOFF + offset
                kept = inside & (abs(offset - REACH) <= reach[source])
                value = jnp.where(kept, quad[at], 0.0)
                which = basis[at]
                hit = diagonal == slot * WINDOW + SHIFT - REACH + step
                band32[which] = band32[which] + jnp.where(hit, value, 0.0)
        band[...] = band32[...].reshape(band.shape).astype(band.dtype)


SMEM = pl.BlockSpec(memory_space=pltpu.SMEM)
VMEM = pl.BlockSpec(memory_space=pltpu.VMEM)
ANY = pl.BlockSpec(memory_space=pl.ANY)
BAND = (K * BLOCK, DEPTH * WINDOW)


def params():
    return pltpu.CompilerParams(vmem_limit_bytes=LIMIT * 1024 * 1024)


def cost(flops):
    return pl.CostEstimate(flops=flops, bytes_accessed=flops // 100, transcendentals=0)


def bands(scalars):
    return pl.pallas_call(
        bands_kernel,
        out_shape=[jax.ShapeDtypeStruct(BAND, jnp.bfloat16)] * 2,
        in_specs=[SMEM] * 6,
        out_specs=[VMEM] * 2,
        scratch_shapes=[pltpu.VMEM((K, BLOCK, DEPTH * WINDOW), jnp.float32)],
        compiler_params=params(),
        name="bands",
    )(*scalars)


def window_copies(counts, pieces, slots, arrived):
    cells = slots.shape[1] - WRAP
    tile = cells // TILES
    groups, used = [], 0
    for part in range(TILES):
        low = part * tile + WRAP if part else 0
        high = (part + 1) * tile + WRAP
        copies = []
        for slot, count in enumerate(counts):
            begin = 0
            moves = []
            for piece in pieces[sum(counts[:slot]) :][:count]:
                end = begin + piece.shape[0]
                first, last = max(low, begin), min(high, end)
                if first < last:
                    moves.append((piece.at[pl.ds(first - begin, last - first)], first))
                if begin == 0 and high > cells:
                    moves.append((piece.at[pl.ds(0, WRAP)], cells))
                begin = end
            for source, at in moves:
                target = slots.at[slot, pl.ds(at, source.shape[0])]
                copies.append(pltpu.make_async_copy(source, target, arrived.at[used]))
                used += 1
        groups.append(copies)
    return groups


def mix(band, slots, mixed, begin, blocks):
    width = slots.shape[2]

    @pl.loop(0, blocks, unroll=15)
    def _(block):
        at = pl.multiple_of(begin + block * BLOCK, BLOCK)
        window = jnp.concatenate([slots[slot, pl.ds(at, WINDOW), :] for slot in range(DEPTH)], axis=0)
        result = jnp.dot(band[...], window, preferred_element_type=jnp.float32).astype(jnp.bfloat16)
        for k in range(K):
            mixed[pl.ds(at, BLOCK), k * width : (k + 1) * width] = result[k * BLOCK : (k + 1) * BLOCK]


def layer_kernel(counts, meta, *refs):
    pieces, refs = refs[: sum(counts)], refs[sum(counts) :]
    *given, mixed, shifted, slots, weights, turned, grad, arrived, fetched = refs
    band, weights_in, *given = given
    turned_in, out, *grads = given if len(given) > 1 else (None, *given)
    cells, width = out.shape
    tile = cells // TILES
    groups = window_copies(counts, pieces, slots, arrived)
    fetches = [pltpu.make_async_copy(weights_in, weights, fetched.at[0])]
    if grads:
        fetches.append(pltpu.make_async_copy(turned_in, turned, fetched.at[1]))
    for copy in groups[0]:
        copy.start()
    for copy in fetches:
        copy.start()
    for copies in groups[1:]:
        for copy in copies:
            copy.start()
    for copies in groups:
        for copy in copies:
            copy.wait()
    mix(band, slots, mixed, 0, cells // BLOCK)
    for copy in fetches:
        copy.wait()
    for part in range(TILES):
        shifted[part * tile + SHIFT : (part + 1) * tile + SHIFT] = jnp.dot(
            mixed[part * tile : (part + 1) * tile], weights[...], preferred_element_type=jnp.float32
        )
    shifted[:SHIFT] = shifted[cells:]
    for part in range(TILES):
        out[part * tile : (part + 1) * tile, :] = shifted[part * tile : (part + 1) * tile].astype(out.dtype)
    if not grads:
        return
    target = grads[0] if len(grads) == 1 else grad
    for k in range(K):
        term = jnp.dot(turned[...], mixed[:, k * width : (k + 1) * width], preferred_element_type=jnp.float32)
        target[k * width : (k + 1) * width, :] = term.T.astype(grad.dtype)
    if len(grads) == 2:
        core = meta[DEPTH] % 2
        lines = grads[0].shape[1]
        for pair in range(grads[0].shape[0]):
            for which, array in enumerate(grads):
                other = core if which == 0 else 1 - core
                at = pl.multiple_of((2 * pair + other) * lines, 16)
                array[pair] = grad[pl.ds(at, lines), :]


def layer(meta, band, slots, weights, devices, turned=None):
    width = weights.shape[1]
    cells = sum(piece.shape[0] for piece in slots[0])
    counts = tuple(len(slot) for slot in slots)
    pieces = [piece for slot in slots for piece in slot]
    lines = K * width // devices
    outs = [jax.ShapeDtypeStruct((cells, width), jnp.bfloat16)]
    operands = [weights]
    if turned is not None:
        operands.append(turned)
        if lines % 16 == 0:
            outs += [jax.ShapeDtypeStruct((devices // 2, lines, width), jnp.bfloat16)] * 2
        else:
            outs += [jax.ShapeDtypeStruct((K * width, width), jnp.bfloat16)]
    out, *grads = pl.pallas_call(
        functools.partial(layer_kernel, counts),
        out_shape=outs,
        in_specs=[SMEM] + [ANY] * len(pieces) + [VMEM] + [ANY] * len(operands),
        out_specs=[VMEM] * len(outs),
        scratch_shapes=[
            pltpu.VMEM((cells, K * width), jnp.bfloat16),
            pltpu.VMEM((cells + SHIFT, width), jnp.float32),
            pltpu.VMEM((DEPTH, cells + WRAP, width), jnp.bfloat16),
            pltpu.VMEM(weights.shape, jnp.bfloat16),
            pltpu.VMEM((width, cells), jnp.bfloat16),
            pltpu.VMEM((K * width, width), jnp.bfloat16),
            pltpu.SemaphoreType.DMA((TILES * 2 * len(pieces),)),
            pltpu.SemaphoreType.DMA((2,)),
        ],
        compiler_params=params(),
        cost_estimate=cost(COST if turned is None else FCOST),
        name="backward_layer" if turned is None else "forward_layer",
    )(meta, *pieces, band, *operands)
    if len(grads) == 1:
        parts = grads[0].reshape(devices // 2, 2, lines, width)
        core = meta[DEPTH] % 2
        grads = [lax.dynamic_index_in_dim(parts, at, 1, keepdims=False) for at in (core, 1 - core)]
    return out, *grads


def shards(signal, cotangent, weights, first_row, last_row, lon_reach, basis_index, quad_weight):
    own_rows, cells, width = signal.shape
    assert own_rows == 1
    devices = lax.axis_size("lat")
    device = lax.axis_index("lat")
    core, side = device % 2, (device // 2) % 2
    across = [(i, i ^ 2) for i in range(devices)]
    cores = [(i, i ^ 1) for i in range(devices)]
    onward = [(i, i + 4) for i in range(devices) if not i & 2 and i + 4 < devices]
    onward += [(i, i - 4) for i in range(devices) if i & 2 and i >= 4]

    def sent(array, pairs):
        return lax.ppermute(array, "lat", pairs)

    meta = jnp.stack(
        [
            jnp.int32(HALO),
            jnp.where(core == 0, HALO + 1, HALO - 1),
            jnp.where(side == 0, 2 * HALO, 0),
            jnp.where(side == 0, 0, 2 * HALO),
            jnp.where(core == 0, HALO - 1, HALO + 1),
            device,
            jnp.int32(devices),
        ]
    ).astype(jnp.int32)
    scalars = [meta, first_row, last_row, lon_reach, basis_index.reshape(-1), quad_weight.reshape(-1)]

    def split(row, cuts):
        edges = [0, *cuts, cells]
        return [row[low:high] for low, high in zip(edges, edges[1:])]

    def swapped(far, farther):
        return [sent(jnp.where(side == core, one, other), cores) for one, other in zip(far, farther)]

    signal, cotangent = signal[0], cotangent[0]
    turned = jnp.roll(cotangent, -SHIFT, 0).T
    weights_back = weights.reshape(K, width, width).swapaxes(1, 2).reshape(K * width, width)

    signal_far = [sent(piece, across) for piece in split(signal, CUTS_F)]
    signal_beside, cotangent_beside = sent(signal, cores), sent(cotangent, cores)
    ready = (turned, weights_back, bands(scalars), meta)
    if CUTS_F:
        signal_far[0], cotangent_sent, ready = lax.optimization_barrier((signal_far[0], cotangent, ready))
        cotangent_far = [sent(piece, across) for piece in split(cotangent_sent, CUTS_B)]
    else:
        cotangent_far = [sent(piece, across) for piece in split(cotangent, CUTS_B)]
        signal_far[0], ready = lax.optimization_barrier((signal_far[0], ready))
    turned, weights_back, (band, band_back), meta = ready
    signal_farther = [sent(piece, onward) for piece in signal_far]
    cotangent_farther = [sent(piece, onward) for piece in cotangent_far]
    if HOLD:
        signal_farther, _ = lax.optimization_barrier((signal_farther, cotangent_far[0]))
    signal_extra = swapped(signal_far, signal_farther)
    signal_rows = [[signal], [signal_beside], signal_far, signal_farther, signal_extra]
    cotangent_rows = [[cotangent], [cotangent_beside], cotangent_far, cotangent_farther, None]

    output, kept, given = layer(meta, band, signal_rows, weights, devices, turned)
    bit = 1
    while True:
        if bit == TIE:
            given, cotangent_rows[3] = lax.optimization_barrier((given, cotangent_rows[3]))
        arrived = sent(given, [(i, i ^ bit) for i in range(devices)])
        share = kept.astype(jnp.float32) + arrived.astype(jnp.float32)
        bit *= 2
        if bit == devices:
            break
        share = share.astype(jnp.bfloat16)
        if bit == TIE * 2 or TIE == 0 and bit == 2:
            cotangent_rows[4] = swapped(cotangent_far, cotangent_rows[3])
            (signal_grad,) = layer(meta, band_back, cotangent_rows, weights_back, devices)
        if bit == LATE:
            share, signal_grad = lax.optimization_barrier((share, signal_grad))
        parts = share.reshape(share.shape[0] // 2, 2, *share.shape[1:])
        part = (device // bit) % 2
        kept = lax.dynamic_index_in_dim(parts, part, 1, keepdims=False)
        given = lax.dynamic_index_in_dim(parts, 1 - part, 1, keepdims=False)
    weight_grad = share[0] * (1.0 / math.sqrt(devices * cells))
    return output[None], signal_grad[None], weight_grad


def solution(mesh):
    rows = P(("ens", "lat"), None, None)
    return jax.shard_map(
        shards,
        mesh=mesh,
        in_specs=(rows, rows, P(), P(), P(), P(), P(), P()),
        out_specs=(rows, rows, P(("ens", "lat"), None)),
        check_vma=False,
    )
```
